32 devices in a mesh: groups: 2 (over x), scen: 16 (over z, y, core).
Axes of the slice: x: 2, y: 2, z: 4, core: 2. Of those that a mesh axis runs over, the one named last changes fastest.
Arguments:
- factors: bfloat16 [512, 1024], P(('groups', 'scen')), parts along dimension 0, may hold values from -6 to 6
- loadings: bfloat16 [65536, 512], P(('groups', 'scen')), parts along dimension 0, may hold values from -6 to 6
- pattern: int32 [512, 4], P(('groups', 'scen')), parts along dimension 0, may hold values from 0 to 7, as said below
- threshold: float32 [65536], P(('groups', 'scen')), parts along dimension 0, may hold values from -3 to -1
- rho: float32 [65536], P(('groups', 'scen')), parts along dimension 0, may hold values from 0.1 to 0.5
- exposure: float32 [65536], P(('groups', 'scen')), parts along dimension 0, may hold values from 1 to 30
- region: int32 [65536], P(('groups', 'scen')), parts along dimension 0, may hold values from 0 to 15
- tail_mask: int32 [512], P('groups'), parts along dimension 0, may hold values from 0 to 1, as said below
- var_index: int32 [2], P('groups'), parts along dimension 0, may hold values from 0 to 255
Outputs:
- region_loss: float32 [16, 512], P(None, ('groups', 'scen')), parts along dimension 1
- contributions: float32 [65536], P(('groups', 'scen')), parts along dimension 0
- var_contributions: float32 [65536], P(('groups', 'scen')), parts along dimension 0
The draws below stay inside these ranges and needn't reach their ends.
There are 2 independent parts, one for each index of `groups`. The reference program is written for one: setup_inputs(seed, part) draws one part's arguments, and reference() takes and returns one part's arrays. A program takes and returns all parts, laid end to end along the dimension named above; each array names one. Nothing has to cross between parts.
Inputs may be any that keep to these rules, and one draw needn't show every extreme that they name: `pattern`: each row names 4 different factor blocks. `tail_mask`: exactly 16 scenarios are marked.
All inputs are finite; a program needn't handle non-finite values.
Results may differ from the reference program's by a relative error of at most 0.0003.
Values may be sent and summed in bfloat16 or wider, within the bound.
No kernel may reach another device: no remote copies, remote signals or barrier semaphores. Data moves between devices by JAX's collectives and lax.ppermute only.
A program may use at most 128 MiB of HBM per device.

```python
import math
import jax
import jax.numpy as jnp
from jax import lax

F = 1024
NB = 4
R = 16
O_DEV = 2048
OBL = 32768
SCEN = 256
TAIL = 16


def draw_pattern(key, part):
    key = jax.random.fold_in(key, 11)
    nblocks = F // 128
    scores = jax.random.randint(key, (OBL // 128, nblocks), 0, 1 << 20) * nblocks + jnp.arange(nblocks, dtype=jnp.int32)[None, :]
    order = jnp.argsort(scores, axis=1)
    return order[:, :NB].astype(jnp.int32)


def draw_tail_mask(key, part):
    key = jax.random.fold_in(key, 23)
    shuffled = jax.random.permutation(key, SCEN)
    return (shuffled < TAIL).astype(jnp.int32)


def with_ends(values, own_key, smallest, largest):
    extent = values.shape
    index_at = [jax.random.randint(jax.random.fold_in(own_key, axis), (), 0, extent[axis]) for axis in range(len(extent))]
    values = values.at[tuple(index_at)].set(smallest)
    longest = extent.index(max(extent))
    index_at[longest] = (index_at[longest] + 1) % extent[longest]
    return values.at[tuple(index_at)].set(largest)


def steps_of(own_key, dims, cuts, low, high):
    factor_of, own = 1.0, jax.random.fold_in(own_key, 6)
    for position, shards_of in cuts:
        heights = jnp.exp(jax.random.uniform(jax.random.fold_in(own, position), (shards_of,), jnp.float32, low / len(cuts), high / len(cuts)))
        factor_of = factor_of * jnp.repeat(heights, dims[position] // shards_of).reshape([-1 if axis == position else 1 for axis in range(len(dims))])
    return factor_of


def scatter_about(own_key, shape, width, most, cuts=(), kind=jnp.bfloat16):
    values = jax.random.normal(own_key, shape, jnp.float32) * width
    if len(cuts) > 0:
        values = steps_of(own_key, shape, cuts, -0.22, 0.18) * values
    return jnp.clip(values, min=-most, max=most).astype(kind)


def setup_inputs(seed: int = 0, part: int = 0) -> dict:
    keys = jax.random.split(jax.random.key(seed), 10)
    part_splits = jax.random.split(jax.random.fold_in(keys[9], part), 10)
    factors = scatter_about(part_splits[0], (SCEN, F), 1.0, 6.0, ((0, 16),))
    loadings = scatter_about(part_splits[1], (OBL, NB * 128), 1.0, 6.0, ((0, 16),))
    pattern = draw_pattern(jax.random.fold_in(jax.random.fold_in(keys[9], part), 71), part)
    threshold = jnp.clip(-3.0 + 2.0 * jax.random.uniform(part_splits[3], (OBL,), jnp.float32) ** steps_of(part_splits[3], (OBL,), ((0, 16),), -0.2, 0.2), -3.0, -1.0)
    rho = jnp.clip(0.1 + 0.4 * jax.random.uniform(part_splits[4], (OBL,), jnp.float32) ** steps_of(part_splits[4], (OBL,), ((0, 16),), -0.2, 0.2), 0.1, 0.5)
    exposure = jnp.clip(jnp.exp(math.log(30.0) - 3.4011974 * jax.random.uniform(part_splits[5], (OBL,), jnp.float32) ** steps_of(part_splits[5], (OBL,), ((0, 16),), -0.2, 0.2)), 1.0, 30.0)
    region = with_ends(jax.random.randint(part_splits[6], (OBL,), 0, R), jax.random.fold_in(part_splits[6], 1), 0, R - 1).astype(jnp.int32)
    tail_mask = draw_tail_mask(jax.random.fold_in(jax.random.fold_in(keys[9], part), 71), part)
    var_index = jax.random.randint(part_splits[8], (1,), 0, SCEN).astype(jnp.int32)
    return dict(factors=factors, loadings=loadings, pattern=pattern, threshold=threshold, rho=rho, exposure=exposure, region=region, tail_mask=tail_mask, var_index=var_index)


def conditional_default_chance(factor_direction_set, factor_rows, block_ids, threshold, rho):
    member_count = factor_direction_set.shape[0] // 128
    block_width = factor_direction_set.shape[1]
    number_of_openings = block_width // 128
    rows = factor_rows.shape[0]
    loading_block_list = factor_direction_set.reshape(member_count, 128, number_of_openings, 128)
    pieces = factor_rows.reshape(rows, factor_rows.shape[1] // 128, 128)
    total = jnp.zeros((member_count, 128, rows), jnp.float32)
    for opening_position in range(number_of_openings):
        chosen = jnp.take(pieces, block_ids[:, opening_position], axis=1)
        total = total + jnp.einsum('bok,pbk->bop', loading_block_list[:, :, opening_position, :].astype(jnp.float32), chosen.astype(jnp.float32))
    score = total.reshape(member_count * 128, rows)
    squares = factor_direction_set.astype(jnp.float32)
    mean_sq = lax.optimization_barrier(jnp.mean(squares * squares, axis=1))
    loading_scale = jnp.sqrt(rho / (block_width * (mean_sq + 1e-06)))
    argument = (threshold[:, None] - loading_scale[:, None] * score) / jnp.sqrt(1.0 - rho)[:, None]
    return 0.5 * jax.scipy.special.erfc(-argument / jnp.sqrt(jnp.float32(2.0)))

def reference(factors, loadings, pattern, threshold, rho, exposure, region, tail_mask, var_index):
    ranks = jnp.cumsum(tail_mask).astype(jnp.int32) - 1
    picked = (tail_mask[:, None] == 1) & (ranks[:, None] == jnp.arange(TAIL, dtype=jnp.int32)[None, :])
    var_column = (jnp.arange(SCEN, dtype=jnp.int32) == var_index[0])[:, None]
    selector = jnp.concatenate([picked, var_column], axis=1).astype(jnp.float32)
    spans = OBL // O_DEV

    def one_span(inputs):
        dirs, ids, thr, shares, expo, regs = inputs
        probs = conditional_default_chance(dirs, factors, ids, thr, shares)
        onehot = (regs[None, :] == jnp.arange(R, dtype=jnp.int32)[:, None]).astype(jnp.float32)
        partial_loss = jnp.dot(onehot, expo[:, None] * probs, precision=lax.Precision.HIGHEST)
        tail_probs = jnp.dot(probs, selector, precision=lax.Precision.HIGHEST)
        return (partial_loss, tail_probs)
    stacked = (loadings.reshape(spans, O_DEV, -1), pattern.reshape(spans, O_DEV // 128, -1), threshold.reshape(spans, O_DEV), rho.reshape(spans, O_DEV), exposure.reshape(spans, O_DEV), region.reshape(spans, O_DEV))
    partials, tail_probs = lax.map(one_span, stacked)
    region_loss = lax.optimization_barrier(jnp.sum(partials, axis=0)) * (R / OBL)
    tail_flat = tail_probs.reshape(OBL, TAIL + 1)
    contributions = exposure * lax.optimization_barrier(jnp.mean(tail_flat[:, :TAIL], axis=1))
    var_contributions = exposure * tail_flat[:, TAIL]
    return (region_loss, contributions, var_contributions)
```

```python
import functools
import math

import jax
import jax.numpy as jnp
from jax import lax
from jax.experimental import pallas as pl
from jax.experimental.pallas import tpu as pltpu
from jax.sharding import PartitionSpec as P

R = 16
BLK = 128
NT = (((1,), (1,)), ((), ()))
TO_U = math.sqrt(math.log2(math.e) / 2.0)
SHIFT = 3.0
Q = (
    0.3388303816318512,
    1.0164676904678345,
    2.8077750205993652,
    6.835119247436523,
    17.085220336914062,
    -1.4560075998306274,
    182.0042724609375,
    -596.1250610351562,
    493.3643493652344,
)


def flipped(p, n):
    out = 0
    step = 1
    while step < n:
        out = 2 * out + (p & 1)
        p //= 2
        step *= 2
    return out


def prepare_kernel(load_ref, thr_ref, rho_ref, expo_ref, region_ref, par_ref, where_ref):
    rows = load_ref.shape[0]
    width = load_ref.shape[1]
    diagonal = lax.broadcasted_iota(jnp.int32, (BLK, BLK), 0) == lax.broadcasted_iota(jnp.int32, (BLK, BLK), 1)
    row_region = lax.broadcasted_iota(jnp.int32, (BLK, BLK), 0) % R
    for b in range(rows // BLK):
        at = slice(b * BLK, (b + 1) * BLK)
        block = load_ref[at, :]
        gram = lax.dot_general(block, block, NT, preferred_element_type=jnp.float32)
        mean_sq = jnp.sum(jnp.where(diagonal, gram, 0.0), axis=0, keepdims=True) * (1.0 / width)
        rho = rho_ref[:, at]
        scale = jnp.sqrt(rho / (width * (mean_sq + 1e-06)))
        to_u = TO_U / jnp.sqrt(1.0 - rho)
        par_ref[0:1, at] = -thr_ref[:, at] * to_u
        par_ref[1:2, at] = scale * to_u
        par_ref[2:3, at] = expo_ref[:, at]
        where_ref[:, at] = (row_region == region_ref[:, at]).astype(jnp.bfloat16)


def prepare(loadings, threshold, rho, exposure, region):
    rows = loadings.shape[0]
    return pl.pallas_call(
        prepare_kernel,
        out_shape=(
            jax.ShapeDtypeStruct((8, rows), jnp.float32),
            jax.ShapeDtypeStruct((BLK, rows), jnp.bfloat16),
        ),
        compiler_params=pltpu.CompilerParams(vmem_limit_bytes=24 << 20),
        cost_estimate=pl.CostEstimate(
            flops=2 * rows * BLK * loadings.shape[1], bytes_accessed=3 * rows * 512, transcendentals=2 * rows
        ),
        name="prepare",
    )(loadings, threshold[None], rho[None], exposure[None], region[None])


def losses_kernel(n, pat_ref, var_ref, own_ref, other_ref, load_ref, par_ref, where_ref, tail_ref, loss_ref, con_ref, varc_ref, fac_ref, acc_ref):
    me = lax.axis_index("scen")
    half = own_ref.shape[0]
    scen = 2 * half
    mine = scen // n
    for p in range(n):
        to = pl.multiple_of((me ^ flipped(p, n)) * mine, mine)
        source = own_ref if p < n // 2 else other_ref
        q = p % (n // 2)
        fac_ref[pl.ds(to, mine), :] = source[q * mine : (q + 1) * mine, :]
    row = lax.broadcasted_iota(jnp.int32, (16, scen), 0)
    column = lax.broadcasted_iota(jnp.int32, (16, scen), 1)
    tail = jnp.where(tail_ref[...] == 1, 1.0, 0.0)
    at_var = jnp.where(column == var_ref[0], 1.0, 0.0)
    marked = jnp.where(row == 0, tail, jnp.where(row == 1, at_var, 0.0)).astype(jnp.bfloat16)
    marked = jnp.concatenate([marked, marked], axis=1)
    acc_ref[...] = jnp.zeros_like(acc_ref)
    slots = load_ref.shape[1] // BLK

    def block(b, carry):
        at = pl.ds(pl.multiple_of(b * BLK, BLK), BLK)
        chosen = [fac_ref[:, pl.ds(pl.multiple_of(pat_ref[b, j] * BLK, BLK), BLK)] for j in range(slots)]
        score = lax.dot_general(
            jnp.concatenate(chosen, axis=1), load_ref[at, :], NT, preferred_element_type=jnp.float32
        )
        u = par_ref[0:1, at] + par_ref[1:2, at] * score
        expo = par_ref[2:3, at]
        d = jnp.abs(u) + SHIFT
        t = pl.reciprocal(d, approx=True)
        t = t * (2.0 - d * t)
        h = jnp.full_like(t, Q[-1])
        for q in Q[-2::-1]:
            h = h * t + q
        small = h * (t * jnp.exp2(-(u * u))) * expo
        lost = jnp.where(u > 0.0, small, expo - small)
        high = lost.astype(jnp.bfloat16)
        low = (lost - high.astype(jnp.float32)).astype(jnp.bfloat16)
        place = where_ref[:, at]
        acc_ref[...] += lax.dot_general(
            jnp.concatenate([high, low], axis=1),
            jnp.concatenate([place, place], axis=1),
            NT,
            preferred_element_type=jnp.float32,
        )
        picked = jnp.dot(marked, jnp.concatenate([high, low], axis=0), preferred_element_type=jnp.float32)
        con_ref[:, at] = picked[0:1, :] * (16.0 / scen)
        varc_ref[:, at] = picked[1:2, :]
        return carry

    lax.fori_loop(0, load_ref.shape[0] // BLK, block, 0, unroll=2)
    groups = BLK // R
    lane = lax.broadcasted_iota(jnp.int32, (scen, BLK), 1) // R
    kept = jnp.where(lane == lax.broadcasted_iota(jnp.int32, (scen, BLK), 0) % groups, acc_ref[...], 0.0)
    loss_ref[...] = jnp.sum(kept.reshape(scen // groups, groups, BLK), axis=1).reshape(loss_ref.shape)


def losses(n, pattern, var_index, own, other, loadings, params, where, tail_mask):
    rows = loadings.shape[0]
    scen = 2 * own.shape[0]
    vmem = pl.BlockSpec(memory_space=pltpu.VMEM)
    smem = pl.BlockSpec(memory_space=pltpu.SMEM)
    return pl.pallas_call(
        functools.partial(losses_kernel, n),
        out_shape=(
            jax.ShapeDtypeStruct((n, scen // n * R // BLK, BLK), jnp.float32),
            jax.ShapeDtypeStruct((1, rows), jnp.float32),
            jax.ShapeDtypeStruct((1, rows), jnp.float32),
        ),
        in_specs=[smem, smem] + [vmem] * 6,
        out_specs=(vmem, vmem, vmem),
        scratch_shapes=[
            pltpu.VMEM((scen, own.shape[1]), jnp.bfloat16),
            pltpu.VMEM((scen, BLK), jnp.float32),
        ],
        compiler_params=pltpu.CompilerParams(vmem_limit_bytes=24 << 20),
        cost_estimate=pl.CostEstimate(
            flops=2 * rows * scen * 512, bytes_accessed=rows * 1024, transcendentals=2 * rows * scen
        ),
        name="losses",
    )(pattern, var_index, own, other, loadings, params, where, tail_mask[None])


def finish_kernel(factor, parts_ref, out_ref):
    mine = out_ref.shape[1]
    groups = BLK // R
    total = jnp.sum(parts_ref[...], axis=0)
    rows = jnp.concatenate(
        [jnp.broadcast_to(total[k : k + 1, :], (groups, BLK)) for k in range(total.shape[0])], axis=0
    )
    lane = lax.broadcasted_iota(jnp.int32, (mine, BLK), 1)
    kept = jnp.where(lane // R == lax.broadcasted_iota(jnp.int32, (mine, BLK), 0) % groups, rows, 0.0)
    lane = lax.broadcasted_iota(jnp.int32, (R, BLK), 1)
    spread = (lane % R == lax.broadcasted_iota(jnp.int32, (R, BLK), 0)).astype(jnp.float32)
    out_ref[...] = factor * lax.dot_general(
        spread, kept, NT, precision=lax.Precision.HIGHEST, preferred_element_type=jnp.float32
    )


def finish(parts, mine, factor):
    return pl.pallas_call(
        functools.partial(finish_kernel, factor),
        out_shape=jax.ShapeDtypeStruct((R, mine), jnp.float32),
        name="finish",
    )(parts)


def local(factors, loadings, pattern, threshold, rho, exposure, region, tail_mask, var_index):
    n = lax.axis_size("scen")
    mine = factors.shape[0]
    rows = loadings.shape[0]

    def swapped(x, step):
        return lax.ppermute(x, "scen", [(i, i ^ step) for i in range(n)])

    params, where = prepare(loadings, threshold, rho, exposure, region)
    held = factors
    step = n // 2
    while step > 1:
        held = jnp.concatenate([held, swapped(held, step)], axis=0)
        step //= 2
    other = swapped(held, 1)
    loss, con, varc = losses(n, pattern, var_index, held, other, loadings, params, where, tail_mask)
    parts = lax.all_to_all(loss, "scen", 0, 0)
    own_loss = finish(parts, mine, R / (rows * n))
    return own_loss, con.reshape(rows), varc.reshape(rows)


def solution(mesh):
    split = ("groups", "scen")
    return jax.shard_map(
        local,
        mesh=mesh,
        in_specs=(
            P(split, None),
            P(split, None),
            P(split, None),
            P(split),
            P(split),
            P(split),
            P(split),
            P("groups"),
            P("groups"),
        ),
        out_specs=(P(None, split), P(split), P(split)),
        check_vma=False,
    )
```

```python
import functools
import math

import jax
import jax.numpy as jnp
from jax import lax
from jax.experimental import pallas as pl
from jax.experimental.pallas import tpu as pltpu
from jax.sharding import PartitionSpec as P

R = 16
BLK = 128
GROUPS = BLK // R
STRIP = 64
NT = (((1,), (1,)), ((), ()))
LOG2E = math.log2(math.e)
FAR = 2.0
SHIFT = 1.7 / math.sqrt(LOG2E)
Q = tuple(
    c / math.sqrt(LOG2E) ** (i + 1)
    for i, c in enumerate(
        (0.3388296961784363, 0.5761929750442505, 0.7263157367706299, 0.5614434480667114, -1.9068398475646973)
    )
)


def flipped(p, n):
    out = 0
    step = 1
    while step < n:
        out = 2 * out + (p & 1)
        p //= 2
        step *= 2
    return out


def prepare_kernel(
    var_ref, load_hbm, thr_hbm, rho_hbm, expo_hbm, region_hbm, tail_hbm, par_ref, where_ref, mark_ref,
    load_ref, thr_ref, rho_ref, expo_ref, region_ref, tail_ref, sems,
):
    rows, width = load_ref.shape
    pairs = (
        (thr_hbm, thr_ref), (rho_hbm, rho_ref), (expo_hbm, expo_ref), (region_hbm, region_ref), (tail_hbm, tail_ref),
    )
    copies = [pltpu.make_async_copy(a, b, sems.at[i]) for i, (a, b) in enumerate(pairs)]
    parts = 4
    piece = rows // parts
    for i in range(parts):
        at = pl.ds(i * piece, piece)
        copies.append(pltpu.make_async_copy(load_hbm.at[at, :], load_ref.at[at, :], sems.at[len(pairs) + i]))
    for copy in copies:
        copy.start()
    for copy in copies[: len(pairs)]:
        copy.wait()
    scen = tail_ref.shape[1]
    diagonal = lax.broadcasted_iota(jnp.int32, (BLK, BLK), 0) == lax.broadcasted_iota(jnp.int32, (BLK, BLK), 1)
    for c in range(scen // BLK):
        at = slice(c * BLK, (c + 1) * BLK)
        tail = jnp.where(tail_ref[:, at] == 1, 1.0, 0.0)
        mark_ref[0, at, :] = jnp.broadcast_to(tail, (BLK, BLK)).T
        scenario = lax.broadcasted_iota(jnp.int32, (BLK, BLK), 0) + c * BLK
        mark_ref[1, at, :] = jnp.where(scenario == var_ref[0:1, :], 1.0, 0.0)
    row_region = lax.broadcasted_iota(jnp.int32, (BLK, rows), 0) % R
    where_ref[...] = jnp.where(row_region == region_ref[...], 1.0, 0.0).astype(jnp.bfloat16)
    par_ref[...] = jnp.zeros_like(par_ref)
    for i in range(parts):
        copies[len(pairs) + i].wait()
        for b in range(i * piece // BLK, (i + 1) * piece // BLK):
            at = slice(b * BLK, (b + 1) * BLK)
            block = load_ref[at, :]
            gram = lax.dot_general(block, block, NT, preferred_element_type=jnp.float32)
            mean_sq = jnp.sum(jnp.where(diagonal, gram, 0.0), axis=0, keepdims=True) * (1.0 / width)
            rho = rho_ref[:, at]
            scale = jnp.sqrt(rho / (width * (mean_sq + 1e-06)))
            to_z = math.sqrt(0.5) / jnp.sqrt(1.0 - rho)
            par_ref[0:1, at] = -thr_ref[:, at] * to_z
            par_ref[1:2, at] = scale * to_z
            par_ref[2:3, at] = expo_ref[:, at]


def prepare(loadings, threshold, rho, exposure, region, tail_mask, var_index):
    rows = loadings.shape[0]
    scen = tail_mask.shape[0]
    hbm = pl.BlockSpec(memory_space=pltpu.HBM)
    return pl.pallas_call(
        prepare_kernel,
        out_shape=(
            jax.ShapeDtypeStruct((8, rows), jnp.float32),
            jax.ShapeDtypeStruct((BLK, rows), jnp.bfloat16),
            jax.ShapeDtypeStruct((2, scen, BLK), jnp.float32),
        ),
        in_specs=[pl.BlockSpec(memory_space=pltpu.VMEM)] + [hbm] * 6,
        scratch_shapes=[
            pltpu.VMEM(loadings.shape, loadings.dtype),
            pltpu.VMEM((1, rows), jnp.float32),
            pltpu.VMEM((1, rows), jnp.float32),
            pltpu.VMEM((1, rows), jnp.float32),
            pltpu.VMEM((1, rows), jnp.int32),
            pltpu.VMEM((1, scen), jnp.int32),
            pltpu.SemaphoreType.DMA((9,)),
        ],
        compiler_params=pltpu.CompilerParams(vmem_limit_bytes=16 << 20),
        cost_estimate=pl.CostEstimate(
            flops=2 * rows * BLK * loadings.shape[1], bytes_accessed=3 * rows * 512, transcendentals=2 * rows
        ),
        name="prepare",
    )(
        jnp.broadcast_to(var_index[None], (8, BLK)),
        *(
            pltpu.with_memory_space_constraint(x, pltpu.HBM)
            for x in (loadings, threshold[None], rho[None], exposure[None], region[None], tail_mask[None])
        ),
    )


def losses_kernel(
    n, pat_hbm, own_ref, other_ref, load_ref, par_ref, where_ref, mark_ref, loss_ref, con_ref, varc_ref,
    pat_ref, fac_ref, score_ref, lost_ref, sem,
):
    fetch = pltpu.make_async_copy(pat_hbm, pat_ref, sem)
    fetch.start()
    me = lax.axis_index("scen")
    scen = fac_ref.shape[0]
    mine = scen // n
    for p in range(n):
        to = pl.multiple_of((me ^ flipped(p, n)) * mine, mine)
        source = own_ref if p < n // 2 else other_ref
        q = p % (n // 2)
        fac_ref[pl.ds(to, mine), :] = source[q * mine : (q + 1) * mine, :]
    fetch.wait()
    rows, width = load_ref.shape
    blocks = rows // BLK
    slots = score_ref.shape[0]

    def score(b):
        chosen = [fac_ref[:, pl.ds(pl.multiple_of(pat_ref[j, b] * BLK, BLK), BLK)] for j in range(width // BLK)]
        score_ref[b % slots] = lax.dot_general(
            jnp.concatenate(chosen, axis=1),
            load_ref[b * BLK : (b + 1) * BLK, :],
            NT,
            preferred_element_type=jnp.float32,
        )

    def weigh(b):
        at = slice(b * BLK, (b + 1) * BLK)
        shift = par_ref[0:1, at]
        scale = par_ref[1:2, at]
        expo = par_ref[2:3, at]
        half = 0.5 * expo
        tails = jnp.zeros((8, BLK), jnp.float32)
        vars_ = jnp.zeros((8, BLK), jnp.float32)
        for c in range(0, scen, STRIP):
            strip = slice(c, c + STRIP)
            z = shift + scale * score_ref[b % slots, strip, :]
            t = pl.reciprocal(z + SHIFT, approx=True)
            h = jnp.full_like(t, Q[-1])
            for q in Q[-2::-1]:
                h = h * t + q
            far = (h * t) * (jnp.exp2((z * z) * -LOG2E) * expo)
            lost = jnp.where(z > FAR, far, half - half * lax.erf(z))
            high = lost.astype(jnp.bfloat16)
            lost_ref[b % slots, strip, 0:BLK] = high
            lost_ref[b % slots, strip, BLK:] = (lost - high.astype(jnp.float32)).astype(jnp.bfloat16)
            tails += jnp.sum((lost * mark_ref[0, strip, :]).reshape(STRIP // 8, 8, BLK), axis=0)
            vars_ += jnp.sum((lost * mark_ref[1, strip, :]).reshape(STRIP // 8, 8, BLK), axis=0)
        con_ref[b : b + 1, :] = jnp.sum(tails, axis=0, keepdims=True) * (16.0 / scen)
        varc_ref[b : b + 1, :] = jnp.sum(vars_, axis=0, keepdims=True)

    def place(b):
        region = where_ref[:, b * BLK : (b + 1) * BLK]
        return lax.dot_general(
            lost_ref[b % slots], jnp.concatenate([region, region], axis=1), NT, preferred_element_type=jnp.float32
        )

    total = jnp.zeros((scen, BLK), jnp.float32)
    for b in range(blocks + 2):
        if b < blocks:
            score(b)
        if 1 <= b <= blocks:
            weigh(b - 1)
        if 2 <= b:
            total += place(b - 2)
    lane = lax.broadcasted_iota(jnp.int32, (scen, BLK), 1) // R
    kept = jnp.where(lane == lax.broadcasted_iota(jnp.int32, (scen, BLK), 0) % GROUPS, total, 0.0)
    loss_ref[...] = jnp.sum(kept.reshape(scen // GROUPS, GROUPS, BLK), axis=1).reshape(loss_ref.shape)


def losses(n, pattern, own, other, loadings, params, where, marks):
    rows = loadings.shape[0]
    scen = 2 * own.shape[0]
    vmem = pl.BlockSpec(memory_space=pltpu.VMEM)
    hbm = pl.BlockSpec(memory_space=pltpu.HBM)
    return pl.pallas_call(
        functools.partial(losses_kernel, n),
        out_shape=(
            jax.ShapeDtypeStruct((n, scen // n // GROUPS, BLK), jnp.float32),
            jax.ShapeDtypeStruct((rows // BLK, BLK), jnp.float32),
            jax.ShapeDtypeStruct((rows // BLK, BLK), jnp.float32),
        ),
        in_specs=[hbm] + [vmem] * 6,
        out_specs=(vmem, vmem, vmem),
        scratch_shapes=[
            pltpu.SMEM((pattern.shape[1], pattern.shape[0]), jnp.int32),
            pltpu.VMEM((scen, own.shape[1]), jnp.bfloat16),
            pltpu.VMEM((3, scen, BLK), jnp.float32),
            pltpu.VMEM((3, scen, 2 * BLK), jnp.bfloat16),
            pltpu.SemaphoreType.DMA,
        ],
        compiler_params=pltpu.CompilerParams(vmem_limit_bytes=24 << 20),
        cost_estimate=pl.CostEstimate(
            flops=2 * rows * scen * 512, bytes_accessed=rows * 1024, transcendentals=3 * rows * scen
        ),
        name="losses",
    )(pltpu.with_memory_space_constraint(pattern.T, pltpu.HBM), own, other, loadings, params, where, marks)


def finish_kernel(factor, parts_ref, out_ref):
    mine = out_ref.shape[1]
    total = jnp.sum(parts_ref[...], axis=0) * factor
    rows = jnp.concatenate(
        [jnp.broadcast_to(total[k : k + 1, :], (GROUPS, BLK)) for k in range(total.shape[0])], axis=0
    )
    lane = lax.broadcasted_iota(jnp.int32, (mine, BLK), 1)
    kept = jnp.where(lane // R == lax.broadcasted_iota(jnp.int32, (mine, BLK), 0) % GROUPS, rows, 0.0)
    lane = lax.broadcasted_iota(jnp.int32, (R, BLK), 1)
    spread = (lane % R == lax.broadcasted_iota(jnp.int32, (R, BLK), 0)).astype(jnp.float32)
    out_ref[...] = lax.dot_general(
        spread, kept, NT, precision=lax.Precision.HIGHEST, preferred_element_type=jnp.float32
    )


def finish(parts, mine, factor):
    return pl.pallas_call(
        functools.partial(finish_kernel, factor),
        out_shape=jax.ShapeDtypeStruct((R, mine), jnp.float32),
        name="finish",
    )(parts)


def local(factors, loadings, pattern, threshold, rho, exposure, region, tail_mask, var_index):
    n = lax.axis_size("scen")
    mine = factors.shape[0]
    rows = loadings.shape[0]

    def swapped(x, step):
        return lax.ppermute(x, "scen", [(i, i ^ step) for i in range(n)])

    step = n // 2
    prepared = prepare(loadings, threshold, rho, exposure, region, tail_mask, var_index)
    far, prepared = lax.optimization_barrier((swapped(factors, step), prepared))
    held = jnp.concatenate([factors, far], axis=0)
    step //= 2
    while step > 1:
        held = jnp.concatenate([held, swapped(held, step)], axis=0)
        step //= 2
    other = swapped(held, 1)
    loss, con, varc = losses(n, pattern, held, other, loadings, *prepared)
    parts = lax.all_to_all(loss, "scen", 0, 0)
    own_loss = finish(parts, mine, R / (rows * n))
    return own_loss, con.reshape(rows), varc.reshape(rows)


def solution(mesh):
    split = ("groups", "scen")
    return jax.shard_map(
        local,
        mesh=mesh,
        in_specs=(
            P(split, None),
            P(split, None),
            P(split, None),
            P(split),
            P(split),
            P(split),
            P(split),
            P("groups"),
            P("groups"),
        ),
        out_specs=(P(None, split), P(split), P(split)),
        check_vma=False,
    )
```

```python
import functools
import math

import jax
import jax.numpy as jnp
from jax import lax
from jax.experimental import pallas as pl
from jax.experimental.pallas import tpu as pltpu
from jax.sharding import PartitionSpec as P

R = 16
BLK = 128
GROUPS = BLK // R
STRIP = 32
TOGETHER = 4
NT = (((1,), (1,)), ((), ()))
LOG2E = math.log2(math.e)
FAR = 2.0
SHIFT = 1.7 / math.sqrt(LOG2E)
Q = tuple(
    c / math.sqrt(LOG2E) ** (i + 1)
    for i, c in enumerate(
        (0.3388296961784363, 0.5761929750442505, 0.7263157367706299, 0.5614434480667114, -1.9068398475646973)
    )
)


def flipped(p, n):
    out = 0
    step = 1
    while step < n:
        out = 2 * out + (p & 1)
        p //= 2
        step *= 2
    return out


def prepare_kernel(
    var_ref, load_hbm, thr_hbm, rho_hbm, expo_hbm, region_hbm, tail_hbm, par_ref, where_ref, mark_ref,
    load_ref, thr_ref, rho_ref, expo_ref, region_ref, tail_ref, sems,
):
    rows, width = load_ref.shape
    pairs = (
        (thr_hbm, thr_ref), (rho_hbm, rho_ref), (expo_hbm, expo_ref), (region_hbm, region_ref), (tail_hbm, tail_ref),
    )
    copies = [pltpu.make_async_copy(a, b, sems.at[i]) for i, (a, b) in enumerate(pairs)]
    parts = 4
    piece = rows // parts
    for i in range(parts):
        at = pl.ds(i * piece, piece)
        copies.append(pltpu.make_async_copy(load_hbm.at[at, :], load_ref.at[at, :], sems.at[len(pairs) + i]))
    for copy in copies:
        copy.start()
    for copy in copies[: len(pairs)]:
        copy.wait()
    scen = tail_ref.shape[1]
    diagonal = lax.broadcasted_iota(jnp.int32, (BLK, BLK), 0) == lax.broadcasted_iota(jnp.int32, (BLK, BLK), 1)
    for c in range(scen // BLK):
        at = slice(c * BLK, (c + 1) * BLK)
        tail = jnp.where(tail_ref[:, at] == 1, 1.0, 0.0)
        mark_ref[0, at, :] = jnp.broadcast_to(tail, (BLK, BLK)).T
        scenario = lax.broadcasted_iota(jnp.int32, (BLK, BLK), 0) + c * BLK
        mark_ref[1, at, :] = jnp.where(scenario == var_ref[0:1, :], 1.0, 0.0)
    row_region = lax.broadcasted_iota(jnp.int32, (R, rows), 0)
    where_ref[...] = jnp.where(row_region == region_ref[...], 1.0, 0.0).astype(jnp.bfloat16)
    par_ref[...] = jnp.zeros_like(par_ref)
    for i in range(parts):
        copies[len(pairs) + i].wait()
        for b in range(i * piece // BLK, (i + 1) * piece // BLK):
            at = slice(b * BLK, (b + 1) * BLK)
            block = load_ref[at, :]
            gram = lax.dot_general(block, block, NT, preferred_element_type=jnp.float32)
            mean_sq = jnp.sum(jnp.where(diagonal, gram, 0.0), axis=0, keepdims=True) * (1.0 / width)
            rho = rho_ref[:, at]
            scale = jnp.sqrt(rho / (width * (mean_sq + 1e-06)))
            to_z = math.sqrt(0.5) / jnp.sqrt(1.0 - rho)
            par_ref[0:1, at] = -thr_ref[:, at] * to_z
            par_ref[1:2, at] = scale * to_z
            par_ref[2:3, at] = expo_ref[:, at]


def prepare(loadings, threshold, rho, exposure, region, tail_mask, var_index):
    rows = loadings.shape[0]
    scen = tail_mask.shape[0]
    hbm = pl.BlockSpec(memory_space=pltpu.HBM)
    return pl.pallas_call(
        prepare_kernel,
        out_shape=(
            jax.ShapeDtypeStruct((8, rows), jnp.float32),
            jax.ShapeDtypeStruct((R, rows), jnp.bfloat16),
            jax.ShapeDtypeStruct((2, scen, BLK), jnp.float32),
        ),
        in_specs=[pl.BlockSpec(memory_space=pltpu.VMEM)] + [hbm] * 6,
        scratch_shapes=[
            pltpu.VMEM(loadings.shape, loadings.dtype),
            pltpu.VMEM((1, rows), jnp.float32),
            pltpu.VMEM((1, rows), jnp.float32),
            pltpu.VMEM((1, rows), jnp.float32),
            pltpu.VMEM((1, rows), jnp.int32),
            pltpu.VMEM((1, scen), jnp.int32),
            pltpu.SemaphoreType.DMA((9,)),
        ],
        compiler_params=pltpu.CompilerParams(vmem_limit_bytes=16 << 20),
        cost_estimate=pl.CostEstimate(
            flops=2 * rows * BLK * loadings.shape[1], bytes_accessed=3 * rows * 512, transcendentals=2 * rows
        ),
        name="prepare",
    )(
        jnp.broadcast_to(var_index[None], (8, BLK)),
        *(
            pltpu.with_memory_space_constraint(x, pltpu.HBM)
            for x in (loadings, threshold[None], rho[None], exposure[None], region[None], tail_mask[None])
        ),
    )


def turn_kernel(load_ref, turned_ref):
    for b in range(turned_ref.shape[0]):
        turned_ref[b] = load_ref[b * BLK : (b + 1) * BLK, :].T


def turn(loadings):
    rows, width = loadings.shape
    vmem = pl.BlockSpec(memory_space=pltpu.VMEM)
    return pl.pallas_call(
        turn_kernel,
        out_shape=jax.ShapeDtypeStruct((rows // BLK, width, BLK), loadings.dtype),
        in_specs=[vmem],
        out_specs=vmem,
        compiler_params=pltpu.CompilerParams(vmem_limit_bytes=16 << 20),
        cost_estimate=pl.CostEstimate(flops=0, bytes_accessed=4 * rows * width, transcendentals=0),
        name="turn",
    )(loadings)


def gathered_from(p, n):
    return 4 * flipped(p, n // 4)


def weigh_kernel(n, last, bits, *refs):
    pat_ref, load_ref, par_ref, where_ref, mark_ref, con_in, var_in, fac_ref = refs[:8]
    earlier, refs = refs[8:-6], refs[-6:]
    loss_ref, con_ref, varc_ref, score_ref, lost_ref, part_ref = refs
    me = lax.axis_index("scen")
    scen = mark_ref.shape[1]
    mine = scen // n
    here = fac_ref.shape[0]
    for p in range(here // mine):
        owner = me ^ (gathered_from(p, n) | bits)
        part_ref[:, p * mine : (p + 1) * mine, :] = mark_ref[:, pl.ds(pl.multiple_of(owner * mine, mine), mine), :]
    blocks, width, _ = load_ref.shape
    slots = score_ref.shape[0]
    batches = lost_ref.shape[0]

    def score(b):
        chosen = [fac_ref[:, pl.ds(pl.multiple_of(pat_ref[j, b] * BLK, BLK), BLK)] for j in range(width // BLK)]
        score_ref[b % slots] = jnp.dot(
            jnp.concatenate(chosen, axis=1), load_ref[b], preferred_element_type=jnp.float32
        )

    def weigh(b):
        at = slice(b * BLK, (b + 1) * BLK)
        to = b % TOGETHER * BLK
        to_low = to + TOGETHER * BLK
        shift = par_ref[0:1, at]
        scale = par_ref[1:2, at]
        expo = par_ref[2:3, at]
        half = 0.5 * expo
        tails = jnp.zeros((8, BLK), jnp.float32)
        vars_ = jnp.zeros((8, BLK), jnp.float32)
        for c in range(0, here, STRIP):
            strip = slice(c, c + STRIP)
            z = shift + scale * score_ref[b % slots, strip, :]
            t = pl.reciprocal(z + SHIFT, approx=True)
            h = jnp.full_like(t, Q[-1])
            for q in Q[-2::-1]:
                h = h * t + q
            far = (h * t) * (jnp.exp2((z * z) * -LOG2E) * expo)
            lost = jnp.where(z > FAR, far, half - half * lax.erf(z))
            high = lost.astype(jnp.bfloat16)
            lost_ref[b // TOGETHER % batches, strip, to : to + BLK] = high
            lost_ref[b // TOGETHER % batches, strip, to_low : to_low + BLK] = (
                lost - high.astype(jnp.float32)
            ).astype(jnp.bfloat16)
            tails += jnp.sum((lost * part_ref[0, strip, :]).reshape(STRIP // 8, 8, BLK), axis=0)
            vars_ += jnp.sum((lost * part_ref[1, strip, :]).reshape(STRIP // 8, 8, BLK), axis=0)
        con_ref[b : b + 1, :] = con_in[b : b + 1, :] + jnp.sum(tails, axis=0, keepdims=True) * (16.0 / scen)
        varc_ref[b : b + 1, :] = var_in[b : b + 1, :] + jnp.sum(vars_, axis=0, keepdims=True)

    def place(batch):
        region = where_ref[:, batch * TOGETHER * BLK : (batch + 1) * TOGETHER * BLK]
        return lax.dot_general(
            lost_ref[batch % batches], jnp.concatenate([region, region], axis=1), NT, preferred_element_type=jnp.float32
        )

    total = jnp.zeros((here, R), jnp.float32)
    for b in range(blocks + 2):
        if b < blocks:
            score(b)
        if 1 <= b <= blocks:
            weigh(b - 1)
        if 2 <= b and (b - 1) % TOGETHER == 0:
            total += place((b - 2) // TOGETHER)
    total = jnp.concatenate([total] * GROUPS, axis=1)
    lane = lax.broadcasted_iota(jnp.int32, (here, BLK), 1) // R
    kept = jnp.where(lane == lax.broadcasted_iota(jnp.int32, (here, BLK), 0) % GROUPS, total, 0.0)
    kept = jnp.sum(kept.reshape(here // GROUPS, GROUPS, BLK), axis=1)
    if not last:
        loss_ref[...] = kept
        return
    high = mine // GROUPS
    for value, first in ((kept, bits), *zip(earlier, last)):
        for p in range(value.shape[0] // high):
            loss_ref[me ^ (gathered_from(p, n) | first)] = value[p * high : (p + 1) * high, :]


def weigh(n, bits, operands, sums, factors, earlier=(), last=()):
    pattern, turned, params, where, marks = operands
    scen = marks.shape[1]
    here = factors.shape[0]
    blocks = turned.shape[0]
    rows = blocks * BLK
    vmem = pl.BlockSpec(memory_space=pltpu.VMEM)
    if last:
        loss = jax.ShapeDtypeStruct((n, scen // n // GROUPS, BLK), jnp.float32)
    else:
        loss = jax.ShapeDtypeStruct((here // GROUPS, BLK), jnp.float32)
    summed = jax.ShapeDtypeStruct((blocks, BLK), jnp.float32)
    operands = (*operands, *sums, factors, *earlier)
    loss, *sums = pl.pallas_call(
        functools.partial(weigh_kernel, n, last, bits),
        out_shape=(loss, summed, summed),
        in_specs=[vmem] * len(operands),
        out_specs=(vmem, vmem, vmem),
        scratch_shapes=[
            pltpu.VMEM((3, here, BLK), jnp.float32),
            pltpu.VMEM((2, here, 2 * TOGETHER * BLK), jnp.bfloat16),
            pltpu.VMEM((2, here, BLK), jnp.float32),
        ],
        compiler_params=pltpu.CompilerParams(vmem_limit_bytes=16 << 20),
        cost_estimate=pl.CostEstimate(
            flops=2 * rows * here * 512, bytes_accessed=rows * 1024, transcendentals=3 * rows * here
        ),
        name=f"weigh{bits}",
    )(*operands)
    return loss, sums


def finish_kernel(factor, parts_ref, con_in, var_in, out_ref, con_ref, varc_ref):
    mine = out_ref.shape[1]
    con_ref[...] = con_in[...]
    varc_ref[...] = var_in[...]
    total = jnp.sum(parts_ref[...], axis=0) * factor
    rows = jnp.concatenate(
        [jnp.broadcast_to(total[k : k + 1, :], (GROUPS, BLK)) for k in range(total.shape[0])], axis=0
    )
    lane = lax.broadcasted_iota(jnp.int32, (mine, BLK), 1)
    kept = jnp.where(lane // R == lax.broadcasted_iota(jnp.int32, (mine, BLK), 0) % GROUPS, rows, 0.0)
    lane = lax.broadcasted_iota(jnp.int32, (R, BLK), 1)
    spread = (lane % R == lax.broadcasted_iota(jnp.int32, (R, BLK), 0)).astype(jnp.float32)
    out_ref[...] = lax.dot_general(
        spread, kept, NT, precision=lax.Precision.HIGHEST, preferred_element_type=jnp.float32
    )


def finish(parts, sums, mine, factor):
    vmem = pl.BlockSpec(memory_space=pltpu.VMEM)
    summed = jax.ShapeDtypeStruct(sums[0].shape, jnp.float32)
    return pl.pallas_call(
        functools.partial(finish_kernel, factor),
        out_shape=(jax.ShapeDtypeStruct((R, mine), jnp.float32), summed, summed),
        in_specs=[vmem] * 3,
        out_specs=(vmem, vmem, vmem),
        compiler_params=pltpu.CompilerParams(vmem_limit_bytes=4 << 20),
        name="finish",
    )(parts, *sums)


def local(factors, loadings, pattern, threshold, rho, exposure, region, tail_mask, var_index):
    n = lax.axis_size("scen")
    mine = factors.shape[0]
    rows = loadings.shape[0]

    def swapped(x, step):
        return lax.ppermute(x, "scen", [(i, i ^ step) for i in range(n)])

    step = n // 2
    prepared = prepare(loadings, threshold, rho, exposure, region, tail_mask, var_index)
    far, prepared = lax.optimization_barrier((swapped(factors, step), prepared))
    held = jnp.concatenate([factors, far], axis=0)
    step //= 2
    while step > 4:
        held = jnp.concatenate([held, swapped(held, step)], axis=0)
        step //= 2
    turned = turn(loadings)
    operands = (pattern.T, turned, *prepared)
    zero = jnp.zeros((rows // BLK, BLK), jnp.float32)

    def after(x, y):
        return lax.optimization_barrier((x, y))

    near = swapped(held, 4)
    first, turned = after(held, turned)
    beside = swapped(first, 1)
    loss0, sums = weigh(n, 0, operands, (zero, zero), held)
    near, sums = after(near, sums)
    held = jnp.concatenate([held, near], axis=0)
    across = swapped(held, 2)
    loss1, sums = weigh(n, 1, operands, sums, beside)
    near, sums = after(near, sums)
    beside = swapped(near, 1)
    loss4, sums = weigh(n, 4, operands, sums, near)
    loss5, sums = weigh(n, 5, operands, sums, beside)
    across, sums = after(across, sums)
    corner = swapped(across, 1)
    loss2, sums = weigh(n, 2, operands, sums, across)
    corner, sums = after(corner, sums)
    loss, sums = weigh(n, 3, operands, sums, corner, (loss0, loss1, loss2, loss4, loss5), (0, 1, 2, 4, 5))
    parts = lax.all_to_all(loss, "scen", 0, 0)
    own_loss, con, varc = finish(parts, sums, mine, R / (rows * n))
    return own_loss, con.reshape(rows), varc.reshape(rows)


def solution(mesh):
    split = ("groups", "scen")
    return jax.shard_map(
        local,
        mesh=mesh,
        in_specs=(
            P(split, None),
            P(split, None),
            P(split, None),
            P(split),
            P(split),
            P(split),
            P(split),
            P("groups"),
            P("groups"),
        ),
        out_specs=(P(None, split), P(split), P(split)),
        check_vma=False,
    )
```

```python
import functools
import math

import jax
import jax.numpy as jnp
from jax import lax
from jax.experimental import pallas as pl
from jax.experimental.pallas import tpu as pltpu
from jax.sharding import PartitionSpec as P

R = 16
BLK = 128
GROUPS = BLK // R
STRIP = 32
COST = pl.CostEstimate(flops=2 * 10**9, bytes_accessed=0, transcendentals=0)
TOGETHER = 4
NT = (((1,), (1,)), ((), ()))
LOG2E = math.log2(math.e)
FAR = 2.0
SHIFT = 1.7 / math.sqrt(LOG2E)
Q = tuple(
    c / math.sqrt(LOG2E) ** (i + 1)
    for i, c in enumerate(
        (0.3388296961784363, 0.5761929750442505, 0.7263157367706299, 0.5614434480667114, -1.9068398475646973)
    )
)


def flipped(p, n):
    out = 0
    step = 1
    while step < n:
        out = 2 * out + (p & 1)
        p //= 2
        step *= 2
    return out


def prepare_kernel(
    var_ref, load_hbm, thr_hbm, rho_hbm, expo_hbm, region_hbm, tail_hbm, load_ref, par_ref, where_ref, mark_ref,
    thr_ref, rho_ref, expo_ref, region_ref, tail_ref, sems,
):
    rows = load_ref.shape[0]
    pairs = (
        (thr_hbm, thr_ref), (rho_hbm, rho_ref), (expo_hbm, expo_ref), (region_hbm, region_ref), (tail_hbm, tail_ref),
    )
    copies = [pltpu.make_async_copy(a, b, sems.at[i]) for i, (a, b) in enumerate(pairs)]
    parts = 4
    for i in range(parts):
        at = pl.ds(i * rows // parts, rows // parts)
        copies.append(pltpu.make_async_copy(load_hbm.at[at, :], load_ref.at[at, :], sems.at[len(pairs) + i]))
    for copy in copies:
        copy.start()
    for copy in copies[: len(pairs)]:
        copy.wait()
    scen = tail_ref.shape[1]
    for c in range(scen // BLK):
        at = slice(c * BLK, (c + 1) * BLK)
        tail = jnp.where(tail_ref[:, at] == 1, 1.0, 0.0)
        mark_ref[0, at, :] = jnp.broadcast_to(tail, (BLK, BLK)).T
        scenario = lax.broadcasted_iota(jnp.int32, (BLK, BLK), 0) + c * BLK
        mark_ref[1, at, :] = jnp.where(scenario == var_ref[0:1, :], 1.0, 0.0)
    row_region = lax.broadcasted_iota(jnp.int32, (R, rows), 0)
    where_ref[...] = jnp.where(row_region == region_ref[...], 1.0, 0.0).astype(jnp.bfloat16)
    par_ref[...] = jnp.zeros_like(par_ref)
    rho = rho_ref[...]
    to_z = math.sqrt(0.5) / jnp.sqrt(1.0 - rho)
    par_ref[0:1, :] = -thr_ref[...] * to_z
    par_ref[1:2, :] = to_z
    par_ref[2:3, :] = expo_ref[...]
    par_ref[3:4, :] = rho
    for copy in copies[len(pairs) :]:
        copy.wait()


def prepare(loadings, threshold, rho, exposure, region, tail_mask, var_index):
    rows = loadings.shape[0]
    scen = tail_mask.shape[0]
    hbm = pl.BlockSpec(memory_space=pltpu.HBM)
    return pl.pallas_call(
        prepare_kernel,
        out_shape=(
            jax.ShapeDtypeStruct(loadings.shape, loadings.dtype),
            jax.ShapeDtypeStruct((8, rows), jnp.float32),
            jax.ShapeDtypeStruct((R, rows), jnp.bfloat16),
            jax.ShapeDtypeStruct((2, scen, BLK), jnp.float32),
        ),
        in_specs=[pl.BlockSpec(memory_space=pltpu.VMEM)] + [hbm] * 6,
        scratch_shapes=[
            pltpu.VMEM((1, rows), jnp.float32),
            pltpu.VMEM((1, rows), jnp.float32),
            pltpu.VMEM((1, rows), jnp.float32),
            pltpu.VMEM((1, rows), jnp.int32),
            pltpu.VMEM((1, scen), jnp.int32),
            pltpu.SemaphoreType.DMA((9,)),
        ],
        compiler_params=pltpu.CompilerParams(vmem_limit_bytes=16 << 20),
        cost_estimate=COST,
        name="prepare",
    )(
        jnp.broadcast_to(var_index[None], (8, BLK)),
        *(
            pltpu.with_memory_space_constraint(x, pltpu.HBM)
            for x in (loadings, threshold[None], rho[None], exposure[None], region[None], tail_mask[None])
        ),
    )


def turn_kernel(load_ref, par_in, turned_ref, par_ref):
    width = load_ref.shape[1]
    diagonal = lax.broadcasted_iota(jnp.int32, (BLK, BLK), 0) == lax.broadcasted_iota(jnp.int32, (BLK, BLK), 1)
    par_ref[...] = par_in[...]
    for b in range(turned_ref.shape[0]):
        at = slice(b * BLK, (b + 1) * BLK)
        block = load_ref[at, :]
        turned = block.T
        turned_ref[b] = turned
        gram = jnp.dot(block, turned, preferred_element_type=jnp.float32)
        mean_sq = jnp.sum(jnp.where(diagonal, gram, 0.0), axis=0, keepdims=True) * (1.0 / width)
        par_ref[1:2, at] = par_in[1:2, at] * jnp.sqrt(par_in[3:4, at] / (width * (mean_sq + 1e-06)))


def turn(loadings, params):
    rows, width = loadings.shape
    vmem = pl.BlockSpec(memory_space=pltpu.VMEM)
    return pl.pallas_call(
        turn_kernel,
        out_shape=(
            jax.ShapeDtypeStruct((rows // BLK, width, BLK), loadings.dtype),
            jax.ShapeDtypeStruct(params.shape, params.dtype),
        ),
        in_specs=[vmem, vmem],
        out_specs=(vmem, vmem),
        compiler_params=pltpu.CompilerParams(vmem_limit_bytes=16 << 20),
        cost_estimate=COST,
        name="turn",
    )(loadings, params)


def gathered_from(p, n):
    q, low = divmod(p, 4)
    return 16 * flipped(q, n // 16) ^ 4 * low


def weigh_kernel(n, last, bits, *refs):
    pat_ref, load_ref, par_ref, where_ref, mark_ref, con_in, var_in, fac_ref = refs[:8]
    earlier, refs = refs[8:-6], refs[-6:]
    loss_ref, con_ref, varc_ref, score_ref, lost_ref, part_ref = refs
    me = lax.axis_index("scen")
    scen = mark_ref.shape[1]
    mine = scen // n
    here = fac_ref.shape[0]
    for p in range(here // mine):
        owner = me ^ (gathered_from(p, n) | bits)
        part_ref[:, p * mine : (p + 1) * mine, :] = mark_ref[:, pl.ds(pl.multiple_of(owner * mine, mine), mine), :]
    blocks, width, _ = load_ref.shape
    slots = score_ref.shape[0]
    batches = lost_ref.shape[0]

    def score(b):
        chosen = [fac_ref[:, pl.ds(pl.multiple_of(pat_ref[j, b] * BLK, BLK), BLK)] for j in range(width // BLK)]
        score_ref[b % slots] = jnp.dot(
            jnp.concatenate(chosen, axis=1), load_ref[b], preferred_element_type=jnp.float32
        )

    def weigh(b):
        at = slice(b * BLK, (b + 1) * BLK)
        to = b % TOGETHER * BLK
        to_low = to + TOGETHER * BLK
        shift = par_ref[0:1, at]
        scale = par_ref[1:2, at]
        expo = par_ref[2:3, at]
        half = 0.5 * expo
        tails = jnp.zeros((8, BLK), jnp.float32)
        vars_ = jnp.zeros((8, BLK), jnp.float32)
        for c in range(0, here, STRIP):
            strip = slice(c, c + STRIP)
            z = shift + scale * score_ref[b % slots, strip, :]
            t = pl.reciprocal(z + SHIFT, approx=True)
            h = jnp.full_like(t, Q[-1])
            for q in Q[-2::-1]:
                h = h * t + q
            far = (h * t) * (jnp.exp2((z * z) * -LOG2E) * expo)
            lost = jnp.where(z > FAR, far, half - half * lax.erf(z))
            high = lost.astype(jnp.bfloat16)
            lost_ref[b // TOGETHER % batches, strip, to : to + BLK] = high
            lost_ref[b // TOGETHER % batches, strip, to_low : to_low + BLK] = (
                lost - high.astype(jnp.float32)
            ).astype(jnp.bfloat16)
            tails += jnp.sum((lost * part_ref[0, strip, :]).reshape(STRIP // 8, 8, BLK), axis=0)
            vars_ += jnp.sum((lost * part_ref[1, strip, :]).reshape(STRIP // 8, 8, BLK), axis=0)
        con_ref[b : b + 1, :] = con_in[b : b + 1, :] + jnp.sum(tails, axis=0, keepdims=True) * (16.0 / scen)
        varc_ref[b : b + 1, :] = var_in[b : b + 1, :] + jnp.sum(vars_, axis=0, keepdims=True)

    def place(batch):
        region = where_ref[:, batch * TOGETHER * BLK : (batch + 1) * TOGETHER * BLK]
        return lax.dot_general(
            lost_ref[batch % batches], jnp.concatenate([region, region], axis=1), NT, preferred_element_type=jnp.float32
        )

    total = jnp.zeros((here, R), jnp.float32)
    for b in range(blocks + 2):
        if b < blocks:
            score(b)
        if 1 <= b <= blocks:
            weigh(b - 1)
        if 2 <= b and (b - 1) % TOGETHER == 0:
            total += place((b - 2) // TOGETHER)
    total = jnp.concatenate([total] * GROUPS, axis=1)
    lane = lax.broadcasted_iota(jnp.int32, (here, BLK), 1) // R
    kept = jnp.where(lane == lax.broadcasted_iota(jnp.int32, (here, BLK), 0) % GROUPS, total, 0.0)
    kept = jnp.sum(kept.reshape(here // GROUPS, GROUPS, BLK), axis=1)
    if not last:
        loss_ref[...] = kept
        return
    high = mine // GROUPS
    for value, first in ((kept, bits), *zip(earlier, last)):
        for p in range(value.shape[0] // high):
            loss_ref[me ^ (gathered_from(p, n) | first)] = value[p * high : (p + 1) * high, :]


def weigh(n, bits, operands, sums, factors, earlier=(), last=()):
    pattern, turned, params, where, marks = operands
    scen = marks.shape[1]
    here = factors.shape[0]
    blocks = turned.shape[0]
    rows = blocks * BLK
    vmem = pl.BlockSpec(memory_space=pltpu.VMEM)
    if last:
        loss = jax.ShapeDtypeStruct((n, scen // n // GROUPS, BLK), jnp.float32)
    else:
        loss = jax.ShapeDtypeStruct((here // GROUPS, BLK), jnp.float32)
    summed = jax.ShapeDtypeStruct((blocks, BLK), jnp.float32)
    operands = (*operands, *sums, factors, *earlier)
    loss, *sums = pl.pallas_call(
        functools.partial(weigh_kernel, n, last, bits),
        out_shape=(loss, summed, summed),
        in_specs=[vmem] * len(operands),
        out_specs=(vmem, vmem, vmem),
        scratch_shapes=[
            pltpu.VMEM((3, here, BLK), jnp.float32),
            pltpu.VMEM((2, here, 2 * TOGETHER * BLK), jnp.bfloat16),
            pltpu.VMEM((2, here, BLK), jnp.float32),
        ],
        compiler_params=pltpu.CompilerParams(vmem_limit_bytes=16 << 20),
        cost_estimate=COST,
        name=f"weigh{bits}",
    )(*operands)
    return loss, sums


def finish_kernel(factor, parts_ref, con_in, var_in, out_ref, con_ref, varc_ref):
    mine = out_ref.shape[1]
    con_ref[...] = con_in[...]
    varc_ref[...] = var_in[...]
    total = jnp.sum(parts_ref[...], axis=0) * factor
    rows = jnp.concatenate(
        [jnp.broadcast_to(total[k : k + 1, :], (GROUPS, BLK)) for k in range(total.shape[0])], axis=0
    )
    lane = lax.broadcasted_iota(jnp.int32, (mine, BLK), 1)
    kept = jnp.where(lane // R == lax.broadcasted_iota(jnp.int32, (mine, BLK), 0) % GROUPS, rows, 0.0)
    lane = lax.broadcasted_iota(jnp.int32, (R, BLK), 1)
    spread = (lane % R == lax.broadcasted_iota(jnp.int32, (R, BLK), 0)).astype(jnp.float32)
    out_ref[...] = lax.dot_general(
        spread, kept, NT, precision=lax.Precision.HIGHEST, preferred_element_type=jnp.float32
    )


def finish(parts, sums, mine, factor):
    vmem = pl.BlockSpec(memory_space=pltpu.VMEM)
    summed = jax.ShapeDtypeStruct(sums[0].shape, jnp.float32)
    return pl.pallas_call(
        functools.partial(finish_kernel, factor),
        out_shape=(jax.ShapeDtypeStruct((R, mine), jnp.float32), summed, summed),
        in_specs=[vmem] * 3,
        out_specs=(vmem, vmem, vmem),
        compiler_params=pltpu.CompilerParams(vmem_limit_bytes=4 << 20),
        name="finish",
    )(parts, *sums)


def local(factors, loadings, pattern, threshold, rho, exposure, region, tail_mask, var_index):
    n = lax.axis_size("scen")
    mine = factors.shape[0]
    rows = loadings.shape[0]

    def swapped(x, step):
        return lax.ppermute(x, "scen", [(i, i ^ step) for i in range(n)])

    def after(x, y):
        return lax.optimization_barrier((x, y))

    held = factors
    step = n // 2
    while step > 8:
        held = jnp.concatenate([held, swapped(held, step)], axis=0)
        step //= 2
    prepared = prepare(loadings, threshold, rho, exposure, region, tail_mask, var_index)
    o8 = swapped(held, 8)
    o12 = swapped(held, 12)
    o4 = swapped(held, 4)
    (o8, o12, o4), prepared = after((o8, o12, o4), prepared)
    others = [o4, o8, o12]
    shape = (-1, 1, mine, factors.shape[1])
    held = jnp.concatenate([x.reshape(shape) for x in (held, *others)], axis=1).reshape(-1, factors.shape[1])
    loadings, params, where, marks = prepared
    turned, params = turn(loadings, params)
    operands = (pattern.T, turned, params, where, marks)
    zero = jnp.zeros((rows // BLK, BLK), jnp.float32)

    across = swapped(held, 2)
    first, turned = after(held, turned)
    beside = swapped(first, 1)
    loss0, sums = weigh(n, 0, operands, (zero, zero), held)
    loss1, sums = weigh(n, 1, operands, sums, beside)
    across, sums = after(across, sums)
    corner = swapped(across, 1)
    loss2, sums = weigh(n, 2, operands, sums, across)
    corner, sums = after(corner, sums)
    loss, sums = weigh(n, 3, operands, sums, corner, (loss0, loss1, loss2), (0, 1, 2))
    parts = lax.all_to_all(loss, "scen", 0, 0)
    own_loss, con, varc = finish(parts, sums, mine, R / (rows * n))
    return own_loss, con.reshape(rows), varc.reshape(rows)


def solution(mesh):
    split = ("groups", "scen")
    return jax.shard_map(
        local,
        mesh=mesh,
        in_specs=(
            P(split, None),
            P(split, None),
            P(split, None),
            P(split),
            P(split),
            P(split),
            P(split),
            P("groups"),
            P("groups"),
        ),
        out_specs=(P(None, split), P(split), P(split)),
        check_vma=False,
    )
```

```python
import functools
import math

import jax
import jax.numpy as jnp
from jax import lax
from jax.experimental import pallas as pl
from jax.experimental.pallas import tpu as pltpu
from jax.sharding import PartitionSpec as P

R = 16
BLK = 128
GROUPS = BLK // R
STRIP = 32
COST = pl.CostEstimate(flops=2 * 10**9, bytes_accessed=0, transcendentals=0)
TOGETHER = 4
NT = (((1,), (1,)), ((), ()))
LOG2E = math.log2(math.e)
FAR = 2.0
SHIFT = 1.7 / math.sqrt(LOG2E)
Q = tuple(
    c / math.sqrt(LOG2E) ** (i + 1)
    for i, c in enumerate(
        (0.3388296961784363, 0.5761929750442505, 0.7263157367706299, 0.5614434480667114, -1.9068398475646973)
    )
)


def flipped(p, n):
    out = 0
    step = 1
    while step < n:
        out = 2 * out + (p & 1)
        p //= 2
        step *= 2
    return out


def prepare_kernel(
    thr_hbm, rho_hbm, expo_hbm, region_hbm, tail_hbm, par_ref, where_ref, mark_ref,
    thr_ref, rho_ref, expo_ref, region_ref, tail_ref, sems,
):
    rows = par_ref.shape[1]
    pairs = (
        (thr_hbm, thr_ref), (rho_hbm, rho_ref), (expo_hbm, expo_ref), (region_hbm, region_ref), (tail_hbm, tail_ref),
    )
    copies = [pltpu.make_async_copy(a, b, sems.at[i]) for i, (a, b) in enumerate(pairs)]
    for copy in copies:
        copy.start()
    for copy in copies:
        copy.wait()
    scen = tail_ref.shape[1]
    for c in range(scen // BLK):
        at = slice(c * BLK, (c + 1) * BLK)
        tail = jnp.where(tail_ref[:, at] == 1, 1.0, 0.0)
        mark_ref[at, :] = jnp.broadcast_to(tail, (BLK, BLK)).T
    row_region = lax.broadcasted_iota(jnp.int32, (R, rows), 0)
    where_ref[...] = jnp.where(row_region == region_ref[...], 1.0, 0.0).astype(jnp.bfloat16)
    par_ref[...] = jnp.zeros_like(par_ref)
    rho = rho_ref[...]
    to_z = math.sqrt(0.5) / jnp.sqrt(1.0 - rho)
    par_ref[0:1, :] = -thr_ref[...] * to_z
    par_ref[1:2, :] = to_z
    par_ref[2:3, :] = expo_ref[...]
    par_ref[3:4, :] = rho


def prepare(threshold, rho, exposure, region, tail_mask):
    rows = threshold.shape[0]
    scen = tail_mask.shape[0]
    hbm = pl.BlockSpec(memory_space=pltpu.HBM)
    return pl.pallas_call(
        prepare_kernel,
        out_shape=(
            jax.ShapeDtypeStruct((8, rows), jnp.float32),
            jax.ShapeDtypeStruct((R, rows), jnp.bfloat16),
            jax.ShapeDtypeStruct((scen, BLK), jnp.float32),
        ),
        in_specs=[hbm] * 5,
        scratch_shapes=[
            pltpu.VMEM((1, rows), jnp.float32),
            pltpu.VMEM((1, rows), jnp.float32),
            pltpu.VMEM((1, rows), jnp.float32),
            pltpu.VMEM((1, rows), jnp.int32),
            pltpu.VMEM((1, scen), jnp.int32),
            pltpu.SemaphoreType.DMA((5,)),
        ],
        compiler_params=pltpu.CompilerParams(vmem_limit_bytes=16 << 20),
        cost_estimate=COST,
        name="prepare",
    )(
        *(
            pltpu.with_memory_space_constraint(x, pltpu.HBM)
            for x in (threshold[None], rho[None], exposure[None], region[None], tail_mask[None])
        ),
    )


def turn_kernel(load_ref, par_in, mark_in, var_ref, turned_ref, par_ref, mark_ref):
    scen = mark_in.shape[0]
    mark_ref[0] = mark_in[...]
    scenario = lax.broadcasted_iota(jnp.int32, (scen, BLK), 0)
    mark_ref[1] = jnp.where(scenario == var_ref[0:1, :], 1.0, 0.0)
    width = load_ref.shape[1]
    diagonal = lax.broadcasted_iota(jnp.int32, (BLK, BLK), 0) == lax.broadcasted_iota(jnp.int32, (BLK, BLK), 1)
    par_ref[...] = par_in[...]
    for b in range(turned_ref.shape[0]):
        at = slice(b * BLK, (b + 1) * BLK)
        block = load_ref[at, :]
        turned = block.T
        turned_ref[b] = turned
        gram = jnp.dot(block, turned, preferred_element_type=jnp.float32)
        mean_sq = jnp.sum(jnp.where(diagonal, gram, 0.0), axis=0, keepdims=True) * (1.0 / width)
        par_ref[1:2, at] = par_in[1:2, at] * jnp.sqrt(par_in[3:4, at] / (width * (mean_sq + 1e-06)))


def turn(loadings, params, marks, var_index):
    rows, width = loadings.shape
    vmem = pl.BlockSpec(memory_space=pltpu.VMEM)
    return pl.pallas_call(
        turn_kernel,
        out_shape=(
            jax.ShapeDtypeStruct((rows // BLK, width, BLK), loadings.dtype),
            jax.ShapeDtypeStruct(params.shape, params.dtype),
            jax.ShapeDtypeStruct((2, *marks.shape), marks.dtype),
        ),
        in_specs=[vmem] * 4,
        out_specs=(vmem, vmem, vmem),
        compiler_params=pltpu.CompilerParams(vmem_limit_bytes=16 << 20),
        cost_estimate=COST,
        name="turn",
    )(loadings, params, marks, jnp.broadcast_to(var_index[None], (8, BLK)))


def gathered_from(p, n):
    q, low = divmod(p, 4)
    return 16 * flipped(q, n // 16) ^ 4 * low


def weigh_kernel(n, last, bits, *refs):
    pat_ref, load_ref, par_ref, where_ref, mark_ref, con_in, var_in, fac_ref = refs[:8]
    earlier, refs = refs[8:-6], refs[-6:]
    loss_ref, con_ref, varc_ref, score_ref, lost_ref, part_ref = refs
    me = lax.axis_index("scen")
    scen = mark_ref.shape[1]
    mine = scen // n
    here = fac_ref.shape[0]
    for p in range(here // mine):
        owner = me ^ (gathered_from(p, n) | bits)
        part_ref[:, p * mine : (p + 1) * mine, :] = mark_ref[:, pl.ds(pl.multiple_of(owner * mine, mine), mine), :]
    blocks, width, _ = load_ref.shape
    slots = score_ref.shape[0]
    batches = lost_ref.shape[0]

    def score(b):
        chosen = [fac_ref[:, pl.ds(pl.multiple_of(pat_ref[j, b] * BLK, BLK), BLK)] for j in range(width // BLK)]
        score_ref[b % slots] = jnp.dot(
            jnp.concatenate(chosen, axis=1), load_ref[b], preferred_element_type=jnp.float32
        )

    def weigh(b):
        at = slice(b * BLK, (b + 1) * BLK)
        to = b % TOGETHER * BLK
        to_low = to + TOGETHER * BLK
        shift = par_ref[0:1, at]
        scale = par_ref[1:2, at]
        expo = par_ref[2:3, at]
        half = 0.5 * expo
        tails = jnp.zeros((8, BLK), jnp.float32)
        vars_ = jnp.zeros((8, BLK), jnp.float32)
        for c in range(0, here, STRIP):
            strip = slice(c, c + STRIP)
            z = shift + scale * score_ref[b % slots, strip, :]
            t = pl.reciprocal(z + SHIFT, approx=True)
            h = jnp.full_like(t, Q[-1])
            for q in Q[-2::-1]:
                h = h * t + q
            far = (h * t) * (jnp.exp2((z * z) * -LOG2E) * expo)
            lost = jnp.where(z > FAR, far, half - half * lax.erf(z))
            high = lost.astype(jnp.bfloat16)
            lost_ref[b // TOGETHER % batches, strip, to : to + BLK] = high
            lost_ref[b // TOGETHER % batches, strip, to_low : to_low + BLK] = (
                lost - high.astype(jnp.float32)
            ).astype(jnp.bfloat16)
            tails += jnp.sum((lost * part_ref[0, strip, :]).reshape(STRIP // 8, 8, BLK), axis=0)
            vars_ += jnp.sum((lost * part_ref[1, strip, :]).reshape(STRIP // 8, 8, BLK), axis=0)
        con_ref[b : b + 1, :] = con_in[b : b + 1, :] + jnp.sum(tails, axis=0, keepdims=True) * (16.0 / scen)
        varc_ref[b : b + 1, :] = var_in[b : b + 1, :] + jnp.sum(vars_, axis=0, keepdims=True)

    def place(batch):
        region = where_ref[:, batch * TOGETHER * BLK : (batch + 1) * TOGETHER * BLK]
        return lax.dot_general(
            lost_ref[batch % batches], jnp.concatenate([region, region], axis=1), NT, preferred_element_type=jnp.float32
        )

    total = jnp.zeros((here, R), jnp.float32)
    for b in range(blocks + 2):
        if b < blocks:
            score(b)
        if 1 <= b <= blocks:
            weigh(b - 1)
        if 2 <= b and (b - 1) % TOGETHER == 0:
            total += place((b - 2) // TOGETHER)
    total = jnp.concatenate([total] * GROUPS, axis=1)
    lane = lax.broadcasted_iota(jnp.int32, (here, BLK), 1) // R
    kept = jnp.where(lane == lax.broadcasted_iota(jnp.int32, (here, BLK), 0) % GROUPS, total, 0.0)
    kept = jnp.sum(kept.reshape(here // GROUPS, GROUPS, BLK), axis=1)
    if not last:
        loss_ref[...] = kept
        return
    high = mine // GROUPS
    for value, first in ((kept, bits), *zip(earlier, last)):
        for p in range(value.shape[0] // high):
            loss_ref[me ^ (gathered_from(p, n) | first)] = value[p * high : (p + 1) * high, :]


def weigh(n, bits, operands, sums, factors, earlier=(), last=()):
    pattern, turned, params, where, marks = operands
    scen = marks.shape[1]
    here = factors.shape[0]
    blocks = turned.shape[0]
    rows = blocks * BLK
    vmem = pl.BlockSpec(memory_space=pltpu.VMEM)
    if last:
        loss = jax.ShapeDtypeStruct((n, scen // n // GROUPS, BLK), jnp.float32)
    else:
        loss = jax.ShapeDtypeStruct((here // GROUPS, BLK), jnp.float32)
    summed = jax.ShapeDtypeStruct((blocks, BLK), jnp.float32)
    operands = (*operands, *sums, factors, *earlier)
    loss, *sums = pl.pallas_call(
        functools.partial(weigh_kernel, n, last, bits),
        out_shape=(loss, summed, summed),
        in_specs=[vmem] * len(operands),
        out_specs=(vmem, vmem, vmem),
        scratch_shapes=[
            pltpu.VMEM((3, here, BLK), jnp.float32),
            pltpu.VMEM((2, here, 2 * TOGETHER * BLK), jnp.bfloat16),
            pltpu.VMEM((2, here, BLK), jnp.float32),
        ],
        compiler_params=pltpu.CompilerParams(vmem_limit_bytes=16 << 20),
        cost_estimate=COST,
        name=f"weigh{bits}",
    )(*operands)
    return loss, sums


def finish_kernel(factor, parts_ref, con_in, var_in, out_ref, con_ref, varc_ref):
    mine = out_ref.shape[1]
    con_ref[...] = con_in[...]
    varc_ref[...] = var_in[...]
    total = jnp.sum(parts_ref[...], axis=0) * factor
    rows = jnp.concatenate(
        [jnp.broadcast_to(total[k : k + 1, :], (GROUPS, BLK)) for k in range(total.shape[0])], axis=0
    )
    lane = lax.broadcasted_iota(jnp.int32, (mine, BLK), 1)
    kept = jnp.where(lane // R == lax.broadcasted_iota(jnp.int32, (mine, BLK), 0) % GROUPS, rows, 0.0)
    lane = lax.broadcasted_iota(jnp.int32, (R, BLK), 1)
    spread = (lane % R == lax.broadcasted_iota(jnp.int32, (R, BLK), 0)).astype(jnp.float32)
    out_ref[...] = lax.dot_general(
        spread, kept, NT, precision=lax.Precision.HIGHEST, preferred_element_type=jnp.float32
    )


def finish(parts, sums, mine, factor):
    vmem = pl.BlockSpec(memory_space=pltpu.VMEM)
    summed = jax.ShapeDtypeStruct(sums[0].shape, jnp.float32)
    return pl.pallas_call(
        functools.partial(finish_kernel, factor),
        out_shape=(jax.ShapeDtypeStruct((R, mine), jnp.float32), summed, summed),
        in_specs=[vmem] * 3,
        out_specs=(vmem, vmem, vmem),
        compiler_params=pltpu.CompilerParams(vmem_limit_bytes=4 << 20),
        name="finish",
    )(parts, *sums)


def local(factors, loadings, pattern, threshold, rho, exposure, region, tail_mask, var_index):
    n = lax.axis_size("scen")
    mine = factors.shape[0]
    rows = loadings.shape[0]

    def swapped(x, step):
        return lax.ppermute(x, "scen", [(i, i ^ step) for i in range(n)])

    def after(x, y):
        return lax.optimization_barrier((x, y))

    held = factors
    step = n // 2
    while step > 8:
        held = jnp.concatenate([held, swapped(held, step)], axis=0)
        step //= 2
    prepared = prepare(threshold, rho, exposure, region, tail_mask)
    z2 = swapped(held, 8)
    z3 = swapped(held, 12)
    z1 = swapped(held, 4)
    y0 = swapped(held, 2)
    (z2, z3, z1), prepared = after((z2, z3, z1), prepared)

    def join(*parts):
        shape = (own.shape[0] // mine, -1, mine, own.shape[1])
        return jnp.concatenate([x.reshape(shape) for x in parts], axis=1).reshape(-1, own.shape[1])

    own = held
    rest = join(z1, z2, z3)
    held = join(own, z1, z2, z3)
    params, where, marks = prepared
    held, (var_index, y0) = after(held, (var_index, y0))
    turned, params, marks = turn(loadings, params, marks, var_index)
    operands = (pattern.T, turned, params, where, marks)
    zero = jnp.zeros((rows // BLK, BLK), jnp.float32)

    across = swapped(rest, 2)
    first, turned = after(held, turned)
    beside = swapped(first, 1)
    loss0, sums = weigh(n, 0, operands, (zero, zero), held)
    loss1, sums = weigh(n, 1, operands, sums, beside)
    across, sums = after(across, sums)
    shape = (own.shape[0] // mine, -1, mine, own.shape[1])
    across = jnp.concatenate([y0.reshape(shape), across.reshape(shape)], axis=1).reshape(-1, own.shape[1])
    corner = swapped(across, 1)
    loss2, sums = weigh(n, 2, operands, sums, across)
    corner, sums = after(corner, sums)
    loss, sums = weigh(n, 3, operands, sums, corner, (loss0, loss1, loss2), (0, 1, 2))
    parts = lax.all_to_all(loss, "scen", 0, 0)
    own_loss, con, varc = finish(parts, sums, mine, R / (rows * n))
    return own_loss, con.reshape(rows), varc.reshape(rows)


def solution(mesh):
    split = ("groups", "scen")
    return jax.shard_map(
        local,
        mesh=mesh,
        in_specs=(
            P(split, None),
            P(split, None),
            P(split, None),
            P(split),
            P(split),
            P(split),
            P(split),
            P("groups"),
            P("groups"),
        ),
        out_specs=(P(None, split), P(split), P(split)),
        check_vma=False,
    )
```
